32 devices in a mesh: row: 4 (over z), col: 8 (over y, x, core).
Axes of the slice: x: 2, y: 2, z: 4, core: 2. Of those that a mesh axis runs over, the one named last changes fastest.
Arguments:
- a_held: float32 [1024, 128, 128], P(('row', 'col')), may hold values from -0.5 to 0.5
- a_slot: int32 [1024], P(('row', 'col')), may hold values from 0 to 1023, as said below
- a_col: int32 [1024], P(('row', 'col')), may hold values from -1 to 15, as said below
- b_held: float32 [2048, 128, 128], P(('row', 'col')), may hold values from -6 to 6
- b_slot: int32 [2048], P(('row', 'col')), may hold values from 0 to 2047, as said below
- b_col: int32 [2048], P(('row', 'col')), may hold values from -1 to 15, as said below
- c_col: int32 [64, 48], P('row', 'col'), may hold values from -1 to 15, as said below
Outputs:
- product: float32 [64, 48, 128, 128], P('row', 'col')
The draws below stay inside these ranges and needn't reach their ends.
Inputs may be any that keep to these rules, and one draw needn't show every extreme that they name: `a_slot`: a permutation of 0 to 1023; one device holds at most 2 slots of one left panel, and some device holds exactly that many. `a_col`: the filled columns of one block row of a left panel are distinct; some block row of every panel has all 4 slots filled. `b_slot`: a permutation of 0 to 2047; one device holds at most 2 slots of one right panel, and some device holds exactly that many. `b_col`: the filled columns of one inner block row of a right panel are distinct; some block row of every panel has all 4 slots filled. `c_col`: the retained columns of one block row within one grid column are distinct, -1 marks an empty slot; every grid column has a block row with all 6 slots retained.
All inputs are finite; a program needn't handle non-finite values.
Results may differ from the reference program's by a relative error of at most 0.0003.
Values sent between devices are 32-bit elements; how exact they have to be, the bound alone decides.
No kernel may reach another device: no remote copies, remote signals or barrier semaphores. Data moves between devices by JAX's collectives and lax.ppermute only.
A program may use at most 192 MiB of HBM per device.

```python
import jax
import jax.numpy as jnp
from jax import lax

BLOCK_EDGE = 128
RB = 16
KPB = 16
CB = 16
WA = 4
WB = 4
WC = 6
STEPS = 3
GRID_ROWS = 4
GRID_COLS = 8
PANELS_A = 16
PANELS_B = 32
SLOTS_A = 64
SLOTS_B = 64
HOLD_A = 32
HOLD_B = 64
DEVICES = 32


def block_pattern(random_seed_key, panel_list, slot_count, row_indices, window_width, window_span, grid_spacing):
    keys = jax.random.split(random_seed_key, 4)
    panel_order = jax.random.permutation(keys[0], panel_list).astype(jnp.int32)
    panel_indices = jnp.arange(panel_list, dtype=jnp.int32)[:, None]
    slot_indices = jnp.arange(slot_count, dtype=jnp.int32)[None, :]
    holder_rank = (grid_spacing * panel_order[:, None] + slot_indices) % (GRID_ROWS * GRID_COLS)
    entry_values = panel_indices * slot_count + slot_indices
    sorting_keys = (holder_rank * (panel_list * slot_count) + entry_values).reshape(-1)
    arrangement = jnp.argsort(sorting_keys, stable=True)
    slot_list = entry_values.reshape(-1)[arrangement].astype(jnp.int32)
    live_count = jax.random.randint(keys[1], (panel_list, row_indices), max(1, window_width - 1), window_width + 1)
    full_row = jax.random.randint(keys[2], (panel_list, 1), 0, row_indices)
    live_count = jnp.where(jnp.arange(row_indices)[None, :] == full_row, window_width, live_count)
    row_keys = jax.random.split(keys[3], panel_list * row_indices)
    chosen = jax.vmap(lambda row_key: jax.random.permutation(row_key, window_span)[:window_width])(row_keys)
    chosen = chosen.reshape(panel_list, row_indices, window_width)
    lane_index = jnp.arange(window_width)[None, None, :]
    column_indices = jnp.where(lane_index < live_count[:, :, None], chosen, -1).astype(jnp.int32).reshape(-1)
    return (slot_list, column_indices[slot_list])


def pattern_left(random_seed_key):
    grid_spacing = GRID_ROWS * GRID_COLS // PANELS_A
    return block_pattern(jax.random.fold_in(random_seed_key, 101), PANELS_A, SLOTS_A, RB, WA, KPB, grid_spacing)


def pattern_right(random_seed_key):
    return block_pattern(jax.random.fold_in(random_seed_key, 202), PANELS_B, SLOTS_B, KPB, WB, CB, 1)


def draw_a_slot(key, part):
    return pattern_left(key)[0]


def draw_a_col(key, part):
    return pattern_left(key)[1]


def draw_b_slot(key, part):
    return pattern_right(key)[0]


def draw_b_col(key, part):
    return pattern_right(key)[1]


def draw_c_col(key, part):
    keys = jax.random.split(jax.random.fold_in(key, 303), 3)
    total_rows = GRID_ROWS * RB
    live_count = jax.random.randint(keys[0], (total_rows, GRID_COLS), 1, WC + 1)
    full_row = jax.random.randint(keys[1], (1, GRID_COLS), 0, RB)
    row_index = jnp.arange(total_rows)[:, None] % RB
    live_count = jnp.where(row_index == full_row, WC, live_count)
    row_keys = jax.random.split(keys[2], total_rows * GRID_COLS)
    chosen = jax.vmap(lambda row_key: jax.random.permutation(row_key, CB)[:WC])(row_keys)
    chosen = chosen.reshape(total_rows, GRID_COLS, WC)
    lane_index = jnp.arange(WC)[None, None, :]
    column_indices = jnp.where(lane_index < live_count[:, :, None], chosen, -1).astype(jnp.int32)
    return column_indices.reshape(total_rows, GRID_COLS * WC)


def levels(rng, extent, shards, least, largest):
    level = 1.0
    for axis_at, shards_of in shards:
        steps = jax.random.uniform(jax.random.fold_in(jax.random.fold_in(rng, 6), axis_at), (shards_of,), jnp.float32, least / len(shards), largest / len(shards))
        level = level * jnp.repeat(jnp.exp(steps), extent[axis_at] // shards_of).reshape((-1,) + (1,) * (len(extent) - 1 - axis_at))
    return level


def normal_values(own_key, shape, spread, limit, shards=(), kind=jnp.bfloat16):
    values = jax.random.normal(own_key, shape, jnp.float32) * spread
    if len(shards) > 0:
        values = levels(own_key, shape, shards, -0.22, 0.18) * values
    return jnp.clip(values, min=-limit, max=limit).astype(kind)


def setup_inputs(seed: int = 0) -> dict:
    splits = jax.random.split(jax.random.key(seed), 8)
    return {
        "a_held": normal_values(splits[0], (DEVICES * HOLD_A, BLOCK_EDGE, BLOCK_EDGE), BLOCK_EDGE ** -0.5, 0.5, ((0, 32),), jnp.float32),
        "a_slot": draw_a_slot(jax.random.fold_in(splits[7], 71), 0),
        "a_col": draw_a_col(jax.random.fold_in(splits[7], 71), 0),
        "b_held": normal_values(splits[3], (DEVICES * HOLD_B, BLOCK_EDGE, BLOCK_EDGE), 1.0, 6.0, ((0, 32),), jnp.float32),
        "b_slot": draw_b_slot(jax.random.fold_in(splits[7], 71), 0),
        "b_col": draw_b_col(jax.random.fold_in(splits[7], 71), 0),
        "c_col": draw_c_col(jax.random.fold_in(splits[7], 71), 0),
    }


def place_every_block(held_blocks, slot_table, column_indices, panel_list, slot_count):
    block_values = jnp.zeros((panel_list * slot_count, BLOCK_EDGE, BLOCK_EDGE), jnp.float32).at[slot_table].set(held_blocks.astype(jnp.float32))
    block_labels = jnp.full((panel_list * slot_count,), -1, jnp.int32).at[slot_table].set(column_indices)
    return block_values, block_labels


def block_terms(left, left_cols, right, right_cols, kept):
    safe = jnp.maximum(left_cols, 0)
    chosen = jnp.take(right, safe, axis=0)
    chosen_cols = jnp.take(right_cols, safe, axis=0)
    pieces = jnp.einsum("rwij,rwvjl->rwvil", left, chosen, precision=lax.Precision.HIGHEST)
    match = (left_cols >= 0)[:, None, :, None] & (chosen_cols[:, None, :, :] == kept[:, :, None, None]) & (kept >= 0)[:, :, None, None]
    return jnp.einsum("rtwv,rwvil->rtil", match.astype(pieces.dtype), pieces, precision=lax.Precision.HIGHEST)


def reference(a_held, a_slot, a_col, b_held, b_slot, b_col, c_col):
    a_vals, a_labels = place_every_block(a_held, a_slot, a_col, PANELS_A, SLOTS_A)
    a_vals = a_vals.reshape(PANELS_A, RB, WA, BLOCK_EDGE, BLOCK_EDGE)
    a_labels = a_labels.reshape(PANELS_A, RB, WA)
    b_vals, b_labels = place_every_block(b_held, b_slot, b_col, PANELS_B, SLOTS_B)
    b_vals = b_vals.reshape(PANELS_B, KPB, WB, BLOCK_EDGE, BLOCK_EDGE)
    b_labels = b_labels.reshape(PANELS_B, KPB, WB)
    retained = c_col.reshape(GRID_ROWS, RB, GRID_COLS, WC).transpose(0, 2, 1, 3)

    def device_tile(position):
        grid_row = position // GRID_COLS
        grid_col = position % GRID_COLS
        kept = retained[grid_row, grid_col]
        accum = jnp.zeros((RB, WC, BLOCK_EDGE, BLOCK_EDGE), a_vals.dtype)
        for iteration in range(STEPS):
            inner = (grid_row + grid_col + iteration) % GRID_ROWS
            left_index = grid_row * GRID_ROWS + inner
            right_index = inner * GRID_COLS + grid_col
            accum = accum + block_terms(a_vals[left_index], a_labels[left_index], b_vals[right_index], b_labels[right_index], kept)
        return accum

    tiles = lax.map(device_tile, jnp.arange(GRID_ROWS * GRID_COLS, dtype=jnp.int32))
    tiles = tiles.reshape(GRID_ROWS, GRID_COLS, RB, WC, BLOCK_EDGE, BLOCK_EDGE).transpose(0, 2, 1, 3, 4, 5)
    return tiles.reshape(GRID_ROWS * RB, GRID_COLS * WC, BLOCK_EDGE, BLOCK_EDGE)
```

```python
import functools

import jax
import jax.numpy as jnp
import numpy as np
from jax import lax
from jax.experimental import pallas as pl
from jax.experimental.pallas import tpu as pltpu
from jax.sharding import PartitionSpec as P

KPB = 16
WA = 4
WB = 4
STEPS = 3
LABEL = 32
ROUNDS = (24,) * 5
LAG = 1
STAGE = 3
FAR = 1 << 16
LOOP_ROUND = 8
SLOTS = 8
VMEM_BYTES = 56 * 2**20


def swap(value, axis, distance):
    if distance == 0:
        return value
    count = lax.axis_size(axis)
    return lax.ppermute(value, axis, [(at, at ^ distance) for at in range(count)])


def share(values):
    count = lax.axis_size("row") * lax.axis_size("col")
    sent = jnp.broadcast_to(values[None], (count,) + values.shape)
    return lax.all_to_all(sent, ("row", "col"), split_axis=0, concat_axis=0, tiled=True)


def pack_order(panel_at, slot, column, places):
    position = jnp.arange(panel_at.shape[0])
    same = (panel_at[:, None] == panel_at[None, :]) & (position[:, None] > position[None, :])
    place = panel_at + jnp.sum(same.astype(jnp.int32), axis=1)
    hit = place[None, :] == jnp.arange(places)[:, None]
    entry = jnp.sum(jnp.where(hit, position[None, :], 0), axis=1)
    label = jnp.sum(jnp.where(hit, (slot * LABEL + column + 2)[None, :], 0), axis=1) - 1
    return entry, label


def split_label(label):
    return jnp.where(label >= 0, label // LABEL, -1), jnp.where(label >= 0, label % LABEL - 1, -1)


def locate(place, bounds):
    part = jnp.zeros(place.shape, jnp.int32)
    offset = place
    for at in range(1, len(bounds) - 1):
        part = part + (place >= int(bounds[at]))
        offset = offset - jnp.where(place >= int(bounds[at]), int(bounds[at] - bounds[at - 1]), 0)
    return part, offset


def flags(condition):
    return condition.astype(jnp.bfloat16)


def starts_of(sizes):
    return np.concatenate([[0], np.cumsum(sizes)]).astype(int)


def available(place, sizes, lag):
    starts = starts_of(sizes)
    ready = jnp.full(place.shape, int(starts[min(lag, len(sizes))]), jnp.int32)
    for at in range(1, len(sizes)):
        gain = int(starts[min(at + lag, len(sizes))] - starts[min(at + lag - 1, len(sizes))])
        if gain:
            ready = ready + jnp.where(place >= int(starts[at]), gain, 0)
    return jnp.where(place >= int(starts[max(len(sizes) - lag, 0)]), FAR, ready)


def one_turn(function, values):
    empty = jax.tree.map(
        lambda part: jnp.zeros(part.shape, part.dtype), jax.eval_shape(function, values)
    )
    turns = 1 + jnp.minimum(jnp.max(values) + 1, 0)
    return lax.fori_loop(0, turns, lambda at, carry: function(values + at), empty)


def queue_places(wanted, origin, ready):
    count, entries = wanted.shape[1:]
    reach = jnp.max(jnp.where(wanted, jnp.arange(count)[None, :, None], -1), axis=1)
    key = ((count - 1 - reach) * count + (count - 1 - origin)) * entries + jnp.arange(entries)
    earlier = key[:, :, None] < key[:, None, :]
    link = jnp.arange(count - 1)[None, :, None]
    item = (origin[:, None] <= link) & (reach[:, None] > link)
    rank = jnp.einsum(
        "dle,def->dlf", flags(item), flags(earlier), preferred_element_type=jnp.float32
    ).astype(jnp.int32)
    upto = earlier | jnp.eye(entries, dtype=bool)[None]
    place = rank[:, 0]
    places = [place]
    for at in range(1, count - 1):
        relayed = item[:, at] & (origin < at)
        behind = jnp.where(relayed, ready(place) - rank[:, at], 0)
        delay = jnp.max(jnp.where(upto, behind[:, :, None], 0), axis=1)
        place = rank[:, at] + delay
        places.append(place)
    return jnp.where(item, jnp.stack(places, axis=1), -1)


def choose(refs, which, use):
    if len(refs) == 1:
        use(refs[0])
        return
    half = len(refs) // 2

    @pl.when(which < half)
    def _():
        choose(refs[:half], which, use)

    @pl.when(which >= half)
    def _():
        choose(refs[half:], which - half, use)


def copy_costs(blocks, edge):
    return pl.CostEstimate(flops=0, bytes_accessed=2 * blocks * edge * edge * 4, transcendentals=0)


def local_params():
    return pltpu.CompilerParams(vmem_limit_bytes=VMEM_BYTES)


def relay(load, outs, buf, load_sem, store_sem):
    total = buf.shape[0]
    lax.fori_loop(
        0, total, lambda at, carry: (load(at, buf.at[at], load_sem.at[at]), carry)[1], 0
    )
    place = 0
    for out in outs:

        def one(at, carry, out=out, place=place):
            pltpu.make_async_copy(
                buf.at[place + at], buf.at[place + at], load_sem.at[place + at]
            ).wait()
            pltpu.make_async_copy(buf.at[place + at], out.at[at], store_sem).start()
            return carry

        lax.fori_loop(0, out.shape[0], one, 0)
        place += out.shape[0]
    for out in outs:
        pltpu.make_async_copy(out, out, store_sem).wait()


def relay_call(kernel, name, codes, sources, sizes):
    block = sources[0].shape[1:]
    total = sum(sizes)
    hbm = pl.BlockSpec(memory_space=pltpu.HBM)
    return pl.pallas_call(
        kernel,
        out_shape=[jax.ShapeDtypeStruct((size,) + block, jnp.float32) for size in sizes],
        in_specs=[pl.BlockSpec(memory_space=pltpu.SMEM)] + [hbm] * len(sources),
        out_specs=[hbm] * len(sizes),
        scratch_shapes=[
            pltpu.VMEM((total,) + block, jnp.float32),
            pltpu.SemaphoreType.DMA((total,)),
            pltpu.SemaphoreType.DMA,
        ],
        compiler_params=local_params(),
        cost_estimate=copy_costs(0, block[0]),
        name=name,
    )(codes, *sources)


def sort_kernel(counts, index_ref, *refs):
    (first, second), outs, (buf, load_sem, store_sem) = refs[:2], refs[2:-3], refs[-3:]

    def load(at, target, sem):
        index = index_ref[at]

        @pl.when(at < counts)
        def _():
            pltpu.make_async_copy(first.at[index], target, sem).start()

        @pl.when(at >= counts)
        def _():
            pltpu.make_async_copy(second.at[index], target, sem).start()

    relay(load, outs, buf, load_sem, store_sem)


def sort_blocks(first, second, first_index, second_index):
    sizes = [index.shape[1] for index in (first_index, second_index) for _ in range(index.shape[0])]
    codes = jnp.concatenate([first_index.reshape(-1), second_index.reshape(-1)])
    kernel = functools.partial(sort_kernel, first_index.size)
    outs = relay_call(kernel, "sort_blocks", codes, [first, second], sizes)
    return list(outs[: first_index.shape[0]]), list(outs[first_index.shape[0] :])


def join_kernel(*refs):
    parts, (out, buf, load_sem, store_sem) = refs[:-4], refs[-4:]
    spans, place = [], 0
    for part in parts:
        spans.append(pl.ds(place, part.shape[0]))
        place += part.shape[0]
    loads = [
        pltpu.make_async_copy(part, buf.at[span], load_sem.at[at])
        for at, (part, span) in enumerate(zip(parts, spans))
    ]
    for load in loads:
        load.start()
    for load, span in zip(loads, spans):
        load.wait()
        pltpu.make_async_copy(buf.at[span], out.at[span], store_sem).start()
    pltpu.make_async_copy(out, out, store_sem).wait()


def join(parts):
    blocks = sum(part.shape[0] for part in parts)
    block = parts[0].shape[1:]
    hbm = pl.BlockSpec(memory_space=pltpu.HBM)
    return pl.pallas_call(
        join_kernel,
        out_shape=jax.ShapeDtypeStruct((blocks,) + block, jnp.float32),
        in_specs=[hbm] * len(parts),
        out_specs=hbm,
        scratch_shapes=[
            pltpu.VMEM((blocks,) + block, jnp.float32),
            pltpu.SemaphoreType.DMA((len(parts),)),
            pltpu.SemaphoreType.DMA,
        ],
        compiler_params=local_params(),
        cost_estimate=copy_costs(blocks, block[0]),
        name="join",
    )(*parts)


def pack_kernel(seen, size, index_ref, *refs):
    sources, outs, (buf, load_sem, store_sem) = refs[:-5], refs[-5:-3], refs[-3:]

    def load(at, target, sem):
        code = index_ref[at]

        def start(ref):
            pltpu.make_async_copy(ref.at[code & 127], target, sem).start()

        for side in range(2):

            @pl.when((at >= side * size) & (at < (side + 1) * size))
            def _():
                arrays = sources[:1] + sources[1 + side * seen : 1 + (side + 1) * seen]
                choose(arrays, lax.shift_right_logical(code, 7), start)

    relay(load, outs, buf, load_sem, store_sem)


def pack_round(codes, own, ups, downs):
    size = codes.shape[1]
    kernel = functools.partial(pack_kernel, len(ups), size)
    return relay_call(kernel, "pack_round", codes.reshape(-1), [own, *ups, *downs], [size, size])


def multiply_kernel(rights, first, list_ref, count_ref, a_ref, *refs):
    b_refs, refs = refs[:rights], refs[rights:]
    if not first:
        c_ref, refs = refs[0], refs[1:]
    out_ref, acc, a_buf, b_buf, a_sem, b_sem, c_sem = refs
    kept = out_ref.shape[0]
    count = count_ref[0]

    def fetch(at):
        @pl.when(at < count)
        def _():
            code = list_ref[at]
            slot = lax.rem(at, SLOTS)
            a_at = lax.shift_right_logical(code, 12) & 2047
            b_off = code & (4095 if rights == 1 else 127)
            pltpu.make_async_copy(a_ref.at[a_at], a_buf.at[slot], a_sem.at[slot]).start()

            def right(ref):
                pltpu.make_async_copy(ref.at[b_off], b_buf.at[slot], b_sem.at[slot]).start()

            choose(b_refs, lax.shift_right_logical(code, 7) & 31, right)

    lax.fori_loop(0, SLOTS, lambda at, carry: (fetch(at), carry)[1], 0)
    if first:

        def clear(at, carry):
            acc[at] = jnp.zeros(acc.shape[1:], jnp.float32)
            return carry

        lax.fori_loop(0, kept, clear, 0)
    else:
        load = pltpu.make_async_copy(c_ref, acc, c_sem)
        load.start()
        load.wait()

    def step(at, carry):
        slot = lax.rem(at, SLOTS)
        pltpu.make_async_copy(a_buf.at[slot], a_buf.at[slot], a_sem.at[slot]).wait()
        pltpu.make_async_copy(b_buf.at[slot], b_buf.at[slot], b_sem.at[slot]).wait()
        a = a_buf[slot]
        b = b_buf[slot]
        a_hi = a.astype(jnp.bfloat16)
        b_hi = b.astype(jnp.bfloat16)
        a_lo = (a - a_hi.astype(jnp.float32)).astype(jnp.bfloat16)
        b_lo = (b - b_hi.astype(jnp.float32)).astype(jnp.bfloat16)
        dot = functools.partial(jnp.dot, preferred_element_type=jnp.float32)
        target = lax.shift_right_logical(list_ref[at], 23)
        acc[target] += dot(a_hi, b_hi) + (dot(a_hi, b_lo) + dot(a_lo, b_hi))
        fetch(at + SLOTS)
        return carry

    lax.fori_loop(0, count, step, 0)
    store = pltpu.make_async_copy(acc, out_ref, c_sem)
    store.start()
    store.wait()


def multiply(codes, count, left, rights, kept, total=None):
    block = left.shape[1:]
    smem = pl.BlockSpec(memory_space=pltpu.SMEM)
    hbm = pl.BlockSpec(memory_space=pltpu.HBM)
    first = total is None
    arrays = [left, *rights] + ([] if first else [total])
    return pl.pallas_call(
        functools.partial(multiply_kernel, len(rights), first),
        out_shape=jax.ShapeDtypeStruct((kept,) + block, jnp.float32),
        in_specs=[smem, smem] + [hbm] * len(arrays),
        out_specs=hbm,
        scratch_shapes=[
            pltpu.VMEM((kept,) + block, jnp.float32),
            pltpu.VMEM((SLOTS,) + block, jnp.float32),
            pltpu.VMEM((SLOTS,) + block, jnp.float32),
            pltpu.SemaphoreType.DMA((SLOTS,)),
            pltpu.SemaphoreType.DMA((SLOTS,)),
            pltpu.SemaphoreType.DMA,
        ],
        compiler_params=local_params(),
        cost_estimate=pl.CostEstimate(
            flops=150 * 6 * block[0] ** 3, bytes_accessed=64 * 2**20, transcendentals=0
        ),
        name="multiply",
    )(codes, count, *arrays)


def hold_kernel(in_ref, out_ref):
    out_ref[...] = in_ref[...]


def hold(values):
    return pl.pallas_call(
        hold_kernel,
        out_shape=jax.ShapeDtypeStruct(values.shape, values.dtype),
        cost_estimate=pl.CostEstimate(flops=0, bytes_accessed=2**28, transcendentals=0),
        name="hold",
    )(values)


def compact(valid, codes):
    candidates = valid.shape[0]
    position = jnp.arange(candidates)
    before = flags(position[:, None] < position[None, :])
    place = jnp.dot(flags(valid)[None], before, preferred_element_type=jnp.float32)[0]
    hit = (place.astype(jnp.int32)[None, :] == position[:, None]) & valid[None, :]
    packed = jnp.sum(jnp.where(hit, codes[None, :], 0), axis=1)
    return packed, jnp.sum(valid.astype(jnp.int32)).reshape(1)


def on_device(a_held, a_slot, a_col, b_held, b_slot, b_col, c_col):
    grid_rows = lax.axis_size("row")
    grid_cols = lax.axis_size("col")
    devices_all = grid_rows * grid_cols
    row = lax.axis_index("row")
    col = lax.axis_index("col")
    rows_dev, retained_width = c_col.shape
    edge = a_held.shape[1]
    slots_left = rows_dev * WA
    slots_right = KPB * WB
    depth_left = max(1, slots_left // devices_all)
    depth_right = max(1, slots_right // devices_all)
    places_left = grid_rows * grid_rows * depth_left
    places_right = grid_cols * grid_rows * depth_right
    rows_at = jnp.arange(grid_rows)

    entry_left, label_left = pack_order(
        a_slot // slots_left * depth_left, a_slot % slots_left, a_col, places_left
    )
    panel_right = b_slot // slots_right
    entry_right, label_right = pack_order(
        (panel_right % grid_cols * grid_rows + panel_right // grid_cols) * depth_right,
        b_slot % slots_right,
        b_col,
        places_right,
    )
    entry_left = jnp.take(entry_left.reshape(grid_rows, -1), row ^ rows_at, axis=0)

    labels = share(jnp.concatenate([label_left, label_right, c_col.reshape(-1)]))

    sent_left, sent_right = sort_blocks(a_held, b_held, entry_left, entry_right[None])
    labels, *sent = lax.optimization_barrier((labels, *sent_left, *sent_right))
    home_right = lax.all_to_all(sent[-1], "col", split_axis=0, concat_axis=0, tiled=True)
    home = [swap(part, "row", at) for at, part in enumerate(sent[:-1])]
    local = home_right.shape[0]

    up = [(at, at + 1) for at in range(grid_rows - 1)]
    down = [(at + 1, at) for at in range(grid_rows - 1)]
    starts = starts_of(ROUNDS)
    capacity = int(starts[-1])
    shape = (grid_rows, grid_rows, grid_cols, depth_right)
    inner_of, origin, from_of, depth_of = (part.reshape(-1) for part in np.indices(shape))
    place_home = jnp.asarray((from_of * grid_rows + inner_of) * depth_right + depth_of, jnp.int32)
    origins = jnp.asarray(np.stack([origin, grid_rows - 1 - origin]), jnp.int32)
    self_at = jnp.stack([row, grid_rows - 1 - row])

    def split_labels(labels):
        left = labels[:, :places_left].reshape(
            grid_rows, grid_cols, grid_rows, grid_rows, depth_left
        )
        right = labels[:, places_left : places_left + places_right].reshape(
            grid_rows, grid_cols, grid_cols, grid_rows, depth_right
        )
        line = lax.dynamic_index_in_dim(right, col, 2, keepdims=False).transpose(2, 0, 1, 3)
        return left, line.reshape(grid_rows, -1)

    def wanted_by_row(labels):
        left, line = split_labels(labels)
        kept = labels[:, places_left + places_right :].reshape(
            grid_rows, grid_cols, rows_dev, retained_width
        )
        kept = lax.dynamic_index_in_dim(kept, col, 1, keepdims=False)
        inner_at = jnp.arange(KPB)
        keeps = flags(jnp.any(kept[:, :, :, None] == inner_at, axis=2))
        slot_a, col_a = split_label(left.transpose(2, 3, 0, 1, 4).reshape(grid_rows, grid_rows, -1))
        by_row = flags((slot_a // WA)[..., None] == jnp.arange(rows_dev))
        by_inner = flags(col_a[..., None] == inner_at)
        has = jnp.einsum("iker,ikeq->ikrq", by_row, by_inner, preferred_element_type=jnp.float32)
        uses = jnp.einsum(
            "ikrq,irj->kqij", has.astype(jnp.bfloat16), keeps, preferred_element_type=jnp.float32
        )
        slot_b, col_b = split_label(line)
        by_slot = flags((slot_b // WB)[..., None] == inner_at)
        found = jnp.einsum(
            "keq,kqij->keij", by_slot, flags(uses > 0.5), preferred_element_type=jnp.float32
        )
        found = jnp.sum(jnp.where(col_b[:, :, None, None] == inner_at, found, 0.0), axis=3)
        in_window = (rows_at[:, None] - rows_at[None, :] - col) % grid_rows < STEPS
        wanted = (found > 0.5) & in_window[:, None, :]
        wanted = wanted.transpose(2, 0, 1).reshape(grid_rows, -1)
        return jnp.stack([wanted, wanted[::-1]])

    def queues(places, capacity, arrived):
        into = jnp.stack(
            [
                lax.dynamic_index_in_dim(places[at], jnp.maximum(self_at[at] - 1, 0), 0, False)
                for at in range(2)
            ]
        )
        outof = jnp.stack(
            [
                lax.dynamic_index_in_dim(
                    places[at], jnp.minimum(self_at[at], grid_rows - 2), 0, False
                )
                for at in range(2)
            ]
        )
        come = jnp.stack(arrived(into))
        source = jnp.where(origins == self_at[:, None], place_home, come)
        hit = outof[:, None, :] == jnp.arange(capacity)[None, :, None]
        send = jnp.sum(jnp.where(hit, source[:, None, :], 0), axis=2)
        send = jnp.where((self_at < grid_rows - 1)[:, None], send, 0)
        lies = jnp.where(origins[0] <= row, source[0], come[1])
        return send, lies

    def products(lies, bounds, stage):
        left, line = split_labels(labels)
        slot_b, col_b = split_label(line)
        inner_at = jnp.arange(KPB)
        where_b = lies.reshape(grid_rows, -1)
        inner = (row + col + jnp.arange(STEPS)) % grid_rows
        slots = jnp.arange(slots_right)
        hit = jnp.take(slot_b, inner, axis=0)[:, None, :] == slots[:, None]
        b_at = jnp.sum(jnp.where(hit, jnp.take(where_b, inner, axis=0)[:, None, :], 0), axis=2)
        b_of = jnp.sum(jnp.where(hit, jnp.take(col_b, inner, axis=0)[:, None, :] + 1, 0), axis=2) - 1
        mine = lax.dynamic_index_in_dim(left, row, 2, keepdims=False)
        mine = jnp.take(mine, row ^ rows_at, axis=0)
        mine = jnp.take(mine, inner, axis=2).transpose(2, 1, 0, 3)
        slot_m, col_m = split_label(mine.reshape(STEPS, -1))
        base = jnp.arange(grid_cols)[:, None] * (places_left + 1)
        base = (base + rows_at * (grid_rows * depth_left)).reshape(1, -1, 1)
        a_place = base + inner[:, None, None] * depth_left + jnp.arange(depth_left)
        a_place = a_place.reshape(STEPS, -1)
        hit = slot_m[:, None, :] == jnp.arange(slots_left)[:, None]
        a_at = jnp.sum(jnp.where(hit, a_place[:, None, :], 0), axis=2)
        a_of = jnp.sum(jnp.where(hit, col_m[:, None, :] + 1, 0), axis=2) - 1
        meets = (a_of[:, :, None] == inner_at)[..., None]
        pair_at = jnp.sum(jnp.where(meets, b_at.reshape(STEPS, 1, KPB, WB), 0), axis=2)
        pair_of = jnp.sum(jnp.where(meets, b_of.reshape(STEPS, 1, KPB, WB) + 1, 0), axis=2) - 1
        kept = jnp.repeat(c_col, WA, axis=0)[None, :, None, :]
        same = (pair_of[..., None] == kept) & (kept >= 0)
        slot = jnp.sum(jnp.where(same, jnp.arange(retained_width) + 1, 0), axis=3) - 1
        target = (jnp.arange(slots_left) // WA)[None, :, None] * retained_width + slot
        left_code = (target * 2**23 + a_at[:, :, None] * 2**12).reshape(-1)
        valid = (slot >= 0).reshape(-1)
        pair_at = pair_at.reshape(-1)
        if bounds is None:
            return [compact(valid, left_code + pair_at)]
        down = pair_at >= local + capacity
        arrived = jnp.where(down, pair_at - capacity, pair_at) - local
        part, offset = locate(arrived, bounds)
        late = (part >= stage) & (arrived >= 0)
        rounds = len(bounds) - 1
        early_code = jnp.where(
            arrived < 0, pair_at, (part + 1 + jnp.where(down, stage, 0)) * 128 + offset
        )
        late_code = (part - stage + jnp.where(down, rounds - stage, 0)) * 128 + offset
        return [
            compact(valid & ~late, left_code + early_code),
            compact(valid & late, left_code + late_code),
        ]

    def plan(labels):
        places = queue_places(
            wanted_by_row(labels), origins, lambda place: available(place, ROUNDS, LAG)
        )
        send, lies = queues(
            places, capacity, lambda into: (local + into[0], local + capacity + into[1])
        )
        send = jnp.where(send >= local + capacity, send - capacity, send)
        part, offset = locate(send - local, starts)
        send = jnp.where(send < local, send, (part + 1) * 128 + offset)
        return send, lies, jnp.max(places) + 1

    send, lies, longest = one_turn(plan, hold(labels))
    longest = jnp.broadcast_to(longest.astype(jnp.float32), (1, edge, edge))
    home_right, send, longest, *home = lax.optimization_barrier((home_right, send, longest, *home))
    home_left = join([*home, longest])
    early, late = products(lies, starts, STAGE)
    left = lax.all_gather(home_left, "col", tiled=True)
    stride = home_left.shape[0]
    longest = jnp.max(left[stride - 1 :: stride, 0, 0]).astype(jnp.int32)
    kept_blocks = rows_dev * retained_width

    def send_round(at, ups, downs):
        seen = max(at - LAG + 1, 0)
        codes = send[:, int(starts[at]) : int(starts[at + 1])]
        go_up, go_down = pack_round(codes, home_right, ups[:seen], downs[:seen])
        return lax.ppermute(go_up, "row", up), lax.ppermute(go_down, "row", down)

    ups, downs = [], []
    for at in range(len(ROUNDS) - 1):
        came_up, came_down = send_round(at, ups, downs)
        ups.append(came_up)
        downs.append(came_down)
    total = multiply(*early, left, [home_right] + ups[:STAGE] + downs[:STAGE], kept_blocks)

    def finished(last_up, last_down):
        rights = [*ups[STAGE:], last_up, *downs[STAGE:], last_down]
        return multiply(*late, left, rights, kept_blocks, total)

    def usual():
        return finished(ups[-1], downs[-1])

    def longer():
        return finished(*send_round(len(ROUNDS) - 1, ups, downs))

    def looped():
        most = min((grid_rows - 1) * local, grid_rows * slots_right) + LOOP_ROUND * grid_rows
        most = -(-most // LOOP_ROUND) * LOOP_ROUND
        shared = most + LOOP_ROUND * (grid_rows + 1)
        end = local + shared
        places = queue_places(
            wanted_by_row(labels), origins, lambda place: (place // LOOP_ROUND + 1) * LOOP_ROUND
        )

        def from_end(place):
            return end - (place // LOOP_ROUND + 1) * LOOP_ROUND + place % LOOP_ROUND

        send, lies = queues(places, most, lambda into: (local + into[0], from_end(into[1])))
        rounds = (lax.pmax(jnp.max(places), ("row", "col")) + LOOP_ROUND) // LOOP_ROUND
        mine = [
            jnp.max(
                lax.dynamic_index_in_dim(places[at], jnp.maximum(self_at[at] - 1, 0), 0, False)
            )
            for at in range(2)
        ]
        mine = [jnp.where(self_at[at] > 0, mine[at], -1) for at in range(2)]
        ((codes, count),) = products(lies, None, None)
        store = jnp.zeros((end + LOOP_ROUND, edge, edge), jnp.float32)
        store = lax.dynamic_update_slice(store, home_right, (0, 0, 0))

        def one(at, store):
            index = lax.dynamic_slice(send, (0, at * LOOP_ROUND), (2, LOOP_ROUND))
            came = [
                lax.ppermute(jnp.take(store, index[side], axis=0, mode="clip"), "row", pairs)
                for side, pairs in ((0, up), (1, down))
            ]
            first = at * LOOP_ROUND
            for side, to in ((0, local + first), (1, end - first - LOOP_ROUND)):
                to = jnp.where(first <= mine[side], to, end)
                store = lax.dynamic_update_slice(store, came[side], (to, 0, 0))
            return store

        store = lax.fori_loop(0, rounds, one, store)
        return multiply(codes, count, left, [store], kept_blocks)

    usual_length = int(starts[-2])
    level = (longest > usual_length).astype(jnp.int32) + (longest > capacity).astype(jnp.int32)
    result = lax.switch(level, [usual, longer, looped])
    return result.reshape(rows_dev, retained_width, edge, edge)


def solution(mesh):
    return jax.shard_map(
        on_device,
        mesh=mesh,
        in_specs=(
            P(("row", "col"), None, None),
            P(("row", "col")),
            P(("row", "col")),
            P(("row", "col"), None, None),
            P(("row", "col")),
            P(("row", "col")),
            P("row", "col"),
        ),
        out_specs=P("row", "col", None, None),
        check_vma=False,
    )
```

```python
import functools

import jax
import jax.numpy as jnp
import numpy as np
from jax import lax
from jax.experimental import pallas as pl
from jax.experimental.pallas import tpu as pltpu
from jax.sharding import PartitionSpec as P

KPB = 16
WA = 4
WB = 4
STEPS = 3
LABEL = 32
ROUNDS = (12,) * 8 + (24,)
LAG = 2
STAGE = 7
FAR = 1 << 16
LOOP_ROUND = 8
SLOTS = 32
GROUP = 8
WEIGHT = 100
VMEM_BYTES = 56 * 2**20


def swap(value, axis, distance):
    if distance == 0:
        return value
    count = lax.axis_size(axis)
    return lax.ppermute(value, axis, [(at, at ^ distance) for at in range(count)])


def share(values):
    count = lax.axis_size("row") * lax.axis_size("col")
    sent = jnp.broadcast_to(values[None], (count,) + values.shape)
    return lax.all_to_all(sent, ("row", "col"), split_axis=0, concat_axis=0, tiled=True)


def pack_order(panel_at, slot, column, places):
    position = jnp.arange(panel_at.shape[0])
    same = (panel_at[:, None] == panel_at[None, :]) & (position[:, None] > position[None, :])
    place = panel_at + jnp.sum(same.astype(jnp.int32), axis=1)
    hit = place[None, :] == jnp.arange(places)[:, None]
    entry = jnp.sum(jnp.where(hit, position[None, :], 0), axis=1)
    label = jnp.sum(jnp.where(hit, (slot * LABEL + column + 2)[None, :], 0), axis=1) - 1
    return entry, label


def split_label(label):
    return jnp.where(label >= 0, label // LABEL, -1), jnp.where(label >= 0, label % LABEL - 1, -1)


def locate(place, bounds):
    part = jnp.zeros(place.shape, jnp.int32)
    offset = place
    for at in range(1, len(bounds) - 1):
        part = part + (place >= int(bounds[at]))
        offset = offset - jnp.where(place >= int(bounds[at]), int(bounds[at] - bounds[at - 1]), 0)
    return part, offset


def flags(condition):
    return condition.astype(jnp.bfloat16)


def starts_of(sizes):
    return np.concatenate([[0], np.cumsum(sizes)]).astype(int)


def available(place, sizes, lag):
    starts = starts_of(sizes)
    ready = jnp.full(place.shape, int(starts[min(lag, len(sizes))]), jnp.int32)
    for at in range(1, len(sizes)):
        gain = int(starts[min(at + lag, len(sizes))] - starts[min(at + lag - 1, len(sizes))])
        if gain:
            ready = ready + jnp.where(place >= int(starts[at]), gain, 0)
    return jnp.where(place >= int(starts[max(len(sizes) - lag, 0)]), FAR, ready)


def one_turn(function, values):
    empty = jax.tree.map(
        lambda part: jnp.zeros(part.shape, part.dtype), jax.eval_shape(function, values)
    )
    turns = 1 + jnp.minimum(jnp.max(values) + 1, 0)
    return lax.fori_loop(0, turns, lambda at, carry: function(values + at), empty)


def queue_places(wanted, origin, ready):
    count, entries = wanted.shape[1:]
    reach = jnp.max(jnp.where(wanted, jnp.arange(count)[None, :, None], -1), axis=1)
    key = ((count - 1 - reach) * count + (count - 1 - origin)) * entries + jnp.arange(entries)
    earlier = key[:, :, None] < key[:, None, :]
    link = jnp.arange(count - 1)[None, :, None]
    item = (origin[:, None] <= link) & (reach[:, None] > link)
    rank = jnp.einsum(
        "dle,def->dlf", flags(item), flags(earlier), preferred_element_type=jnp.float32
    ).astype(jnp.int32)
    upto = earlier | jnp.eye(entries, dtype=bool)[None]
    place = rank[:, 0]
    places = [place]
    for at in range(1, count - 1):
        relayed = item[:, at] & (origin < at)
        behind = jnp.where(relayed, ready(place) - rank[:, at], 0)
        delay = jnp.max(jnp.where(upto, behind[:, :, None], 0), axis=1)
        place = rank[:, at] + delay
        places.append(place)
    return jnp.where(item, jnp.stack(places, axis=1), -1)


def choose(refs, which, use):
    if len(refs) == 1:
        use(refs[0])
        return
    half = len(refs) // 2

    @pl.when(which < half)
    def _():
        choose(refs[:half], which, use)

    @pl.when(which >= half)
    def _():
        choose(refs[half:], which - half, use)


def copy_costs(blocks, edge):
    return pl.CostEstimate(flops=0, bytes_accessed=2 * blocks * edge * edge * 4, transcendentals=0)


def local_params():
    return pltpu.CompilerParams(vmem_limit_bytes=VMEM_BYTES)


def relay(load, outs, buf, load_sem, store_sem):
    total = buf.shape[0]
    lax.fori_loop(
        0, total, lambda at, carry: (load(at, buf.at[at], load_sem.at[at]), carry)[1], 0
    )
    place = 0
    for out in outs:

        def one(at, carry, out=out, place=place):
            pltpu.make_async_copy(
                buf.at[place + at], buf.at[place + at], load_sem.at[place + at]
            ).wait()
            pltpu.make_async_copy(buf.at[place + at], out.at[at], store_sem).start()
            return carry

        lax.fori_loop(0, out.shape[0], one, 0)
        place += out.shape[0]
    for out in outs:
        pltpu.make_async_copy(out, out, store_sem).wait()


def relay_call(kernel, name, codes, sources, sizes, weight=0):
    block = sources[0].shape[1:]
    total = sum(sizes)
    hbm = pl.BlockSpec(memory_space=pltpu.HBM)
    return pl.pallas_call(
        kernel,
        out_shape=[jax.ShapeDtypeStruct((size,) + block, jnp.float32) for size in sizes],
        in_specs=[pl.BlockSpec(memory_space=pltpu.SMEM)] + [hbm] * len(sources),
        out_specs=[hbm] * len(sizes),
        scratch_shapes=[
            pltpu.VMEM((total,) + block, jnp.float32),
            pltpu.SemaphoreType.DMA((total,)),
            pltpu.SemaphoreType.DMA,
        ],
        compiler_params=local_params(),
        cost_estimate=copy_costs(weight, block[0]),
        name=name,
    )(codes, *sources)


def sort_kernel(counts, index_ref, *refs):
    (first, second), outs, (buf, load_sem, store_sem) = refs[:2], refs[2:-3], refs[-3:]

    def load(at, target, sem):
        index = index_ref[at]

        @pl.when(at < counts)
        def _():
            pltpu.make_async_copy(first.at[index], target, sem).start()

        @pl.when(at >= counts)
        def _():
            pltpu.make_async_copy(second.at[index], target, sem).start()

    relay(load, outs, buf, load_sem, store_sem)


def sort_blocks(first, second, first_index, second_index):
    sizes = [index.shape[1] for index in (first_index, second_index) for _ in range(index.shape[0])]
    codes = jnp.concatenate([first_index.reshape(-1), second_index.reshape(-1)])
    kernel = functools.partial(sort_kernel, first_index.size)
    outs = relay_call(kernel, "sort_blocks", codes, [first, second], sizes)
    return list(outs[: first_index.shape[0]]), list(outs[first_index.shape[0] :])


def join_kernel(*refs):
    parts, (out, buf, load_sem, store_sem) = refs[:-4], refs[-4:]
    spans, place = [], 0
    for part in parts:
        spans.append(pl.ds(place, part.shape[0]))
        place += part.shape[0]
    loads = [
        pltpu.make_async_copy(part, buf.at[span], load_sem.at[at])
        for at, (part, span) in enumerate(zip(parts, spans))
    ]
    for load in loads:
        load.start()
    for load, span in zip(loads, spans):
        load.wait()
        pltpu.make_async_copy(buf.at[span], out.at[span], store_sem).start()
    pltpu.make_async_copy(out, out, store_sem).wait()


def join(parts):
    blocks = sum(part.shape[0] for part in parts)
    block = parts[0].shape[1:]
    hbm = pl.BlockSpec(memory_space=pltpu.HBM)
    return pl.pallas_call(
        join_kernel,
        out_shape=jax.ShapeDtypeStruct((blocks,) + block, jnp.float32),
        in_specs=[hbm] * len(parts),
        out_specs=hbm,
        scratch_shapes=[
            pltpu.VMEM((blocks,) + block, jnp.float32),
            pltpu.SemaphoreType.DMA((len(parts),)),
            pltpu.SemaphoreType.DMA,
        ],
        compiler_params=local_params(),
        cost_estimate=copy_costs(blocks, block[0]),
        name="join",
    )(*parts)


def pack_kernel(seen, size, index_ref, *refs):
    sources, outs, (buf, load_sem, store_sem) = refs[:-5], refs[-5:-3], refs[-3:]

    def load(at, target, sem):
        code = index_ref[at]

        def start(ref):
            pltpu.make_async_copy(ref.at[code & 127], target, sem).start()

        for side in range(2):

            @pl.when((at >= side * size) & (at < (side + 1) * size))
            def _():
                arrays = sources[:1] + sources[1 + side * seen : 1 + (side + 1) * seen]
                choose(arrays, lax.shift_right_logical(code, 7), start)

    relay(load, outs, buf, load_sem, store_sem)


def pack_round(codes, own, ups, downs, weight):
    size = codes.shape[1]
    kernel = functools.partial(pack_kernel, len(ups), size)
    return relay_call(kernel, "pack_round", codes.reshape(-1), [own, *ups, *downs], [size, size], weight)


def multiply_kernel(rights, first, list_ref, count_ref, a_ref, *refs):
    b_refs, refs = refs[:rights], refs[rights:]
    if not first:
        c_ref, refs = refs[0], refs[1:]
    out_ref, acc, a_buf, b_buf, a_sem, b_sem, c_sem = refs
    kept = out_ref.shape[0]
    count = count_ref[0]

    def fetch(at):
        @pl.when(at < count)
        def _():
            code = list_ref[at]
            slot = lax.rem(at, SLOTS)
            a_at = lax.shift_right_logical(code, 12) & 2047
            b_off = code & (4095 if rights == 1 else 127)
            pltpu.make_async_copy(a_ref.at[a_at], a_buf.at[slot], a_sem.at[slot]).start()

            def right(ref):
                pltpu.make_async_copy(ref.at[b_off], b_buf.at[slot], b_sem.at[slot]).start()

            choose(b_refs, lax.shift_right_logical(code, 7) & 31, right)

    lax.fori_loop(0, SLOTS, lambda at, carry: (fetch(at), carry)[1], 0)
    if first:

        def clear(at, carry):
            acc[at] = jnp.zeros(acc.shape[1:], jnp.float32)
            return carry

        lax.fori_loop(0, kept, clear, 0)
    else:
        load = pltpu.make_async_copy(c_ref, acc.at[pl.ds(0, kept)], c_sem)
        load.start()
        load.wait()

    def step(group, carry):
        first_at = group * GROUP
        for at in range(GROUP):
            slot = lax.rem(first_at + at, SLOTS)
            pltpu.make_async_copy(a_buf.at[slot], a_buf.at[slot], a_sem.at[slot]).wait()
            pltpu.make_async_copy(b_buf.at[slot], b_buf.at[slot], b_sem.at[slot]).wait()
        results = []
        for at in range(GROUP):
            slot = lax.rem(first_at + at, SLOTS)
            a = a_buf[slot]
            b = b_buf[slot]
            a_hi = a.astype(jnp.bfloat16)
            b_hi = b.astype(jnp.bfloat16)
            a_lo = (a - a_hi.astype(jnp.float32)).astype(jnp.bfloat16)
            b_lo = (b - b_hi.astype(jnp.float32)).astype(jnp.bfloat16)
            results.append(
                jnp.dot(
                    jnp.concatenate([a_hi, a_lo, a_hi], axis=1),
                    jnp.concatenate([b_hi, b_hi, b_lo], axis=0),
                    preferred_element_type=jnp.float32,
                )
            )
        for at in range(GROUP):
            acc[lax.shift_right_logical(list_ref[first_at + at], 23)] += results[at]
        for at in range(GROUP):
            fetch(first_at + at + SLOTS)
        return carry

    lax.fori_loop(0, count // GROUP, step, 0)
    store = pltpu.make_async_copy(acc.at[pl.ds(0, kept)], out_ref, c_sem)
    store.start()
    store.wait()


def multiply(codes, count, left, rights, kept, total=None):
    block = left.shape[1:]
    smem = pl.BlockSpec(memory_space=pltpu.SMEM)
    hbm = pl.BlockSpec(memory_space=pltpu.HBM)
    first = total is None
    arrays = [left, *rights] + ([] if first else [total])
    return pl.pallas_call(
        functools.partial(multiply_kernel, len(rights), first),
        out_shape=jax.ShapeDtypeStruct((kept,) + block, jnp.float32),
        in_specs=[smem, smem] + [hbm] * len(arrays),
        out_specs=hbm,
        scratch_shapes=[
            pltpu.VMEM((kept + 1,) + block, jnp.float32),
            pltpu.VMEM((SLOTS,) + block, jnp.float32),
            pltpu.VMEM((SLOTS,) + block, jnp.float32),
            pltpu.SemaphoreType.DMA((SLOTS,)),
            pltpu.SemaphoreType.DMA((SLOTS,)),
            pltpu.SemaphoreType.DMA,
        ],
        compiler_params=local_params(),
        cost_estimate=pl.CostEstimate(
            flops=150 * 6 * block[0] ** 3, bytes_accessed=64 * 2**20, transcendentals=0
        ),
        name="multiply",
    )(codes, count, *arrays)


def hold_kernel(in_ref, out_ref):
    out_ref[...] = in_ref[...]


def hold(values):
    return pl.pallas_call(
        hold_kernel,
        out_shape=jax.ShapeDtypeStruct(values.shape, values.dtype),
        cost_estimate=pl.CostEstimate(flops=0, bytes_accessed=2**28, transcendentals=0),
        name="hold",
    )(values)


def compact(valid, codes, spare):
    candidates = valid.shape[0]
    position = jnp.arange(candidates)
    before = flags(position[:, None] < position[None, :])
    place = jnp.dot(flags(valid)[None], before, preferred_element_type=jnp.float32)[0]
    listed = jnp.arange(-(-candidates // GROUP) * GROUP)
    hit = (place.astype(jnp.int32)[None, :] == listed[:, None]) & valid[None, :]
    packed = jnp.sum(jnp.where(hit, codes[None, :] - spare, 0), axis=1) + spare
    count = jnp.sum(valid.astype(jnp.int32))
    return packed, ((count + GROUP - 1) // GROUP * GROUP).reshape(1)


def on_device(a_held, a_slot, a_col, b_held, b_slot, b_col, c_col):
    grid_rows = lax.axis_size("row")
    grid_cols = lax.axis_size("col")
    devices_all = grid_rows * grid_cols
    row = lax.axis_index("row")
    col = lax.axis_index("col")
    rows_dev, retained_width = c_col.shape
    edge = a_held.shape[1]
    slots_left = rows_dev * WA
    slots_right = KPB * WB
    depth_left = max(1, slots_left // devices_all)
    depth_right = max(1, slots_right // devices_all)
    places_left = grid_rows * grid_rows * depth_left
    places_right = grid_cols * grid_rows * depth_right
    rows_at = jnp.arange(grid_rows)

    entry_left, label_left = pack_order(
        a_slot // slots_left * depth_left, a_slot % slots_left, a_col, places_left
    )
    panel_right = b_slot // slots_right
    entry_right, label_right = pack_order(
        (panel_right % grid_cols * grid_rows + panel_right // grid_cols) * depth_right,
        b_slot % slots_right,
        b_col,
        places_right,
    )
    entry_left = jnp.take(entry_left.reshape(grid_rows, -1), row ^ rows_at, axis=0)

    labels = share(jnp.concatenate([label_left, label_right, c_col.reshape(-1)]))

    sent_left, sent_right = sort_blocks(a_held, b_held, entry_left, entry_right[None])
    labels, *sent = lax.optimization_barrier((labels, *sent_left, *sent_right))
    home_right = lax.all_to_all(sent[-1], "col", split_axis=0, concat_axis=0, tiled=True)
    home = [swap(part, "row", at) for at, part in enumerate(sent[:-1])]
    local = home_right.shape[0]

    up = [(at, at + 1) for at in range(grid_rows - 1)]
    down = [(at + 1, at) for at in range(grid_rows - 1)]
    starts = starts_of(ROUNDS)
    capacity = int(starts[-1])
    shape = (grid_rows, grid_rows, grid_cols, depth_right)
    inner_of, origin, from_of, depth_of = (part.reshape(-1) for part in np.indices(shape))
    place_home = jnp.asarray((from_of * grid_rows + inner_of) * depth_right + depth_of, jnp.int32)
    origins = jnp.asarray(np.stack([origin, grid_rows - 1 - origin]), jnp.int32)
    self_at = jnp.stack([row, grid_rows - 1 - row])

    def split_labels(labels):
        left = labels[:, :places_left].reshape(
            grid_rows, grid_cols, grid_rows, grid_rows, depth_left
        )
        right = labels[:, places_left : places_left + places_right].reshape(
            grid_rows, grid_cols, grid_cols, grid_rows, depth_right
        )
        line = lax.dynamic_index_in_dim(right, col, 2, keepdims=False).transpose(2, 0, 1, 3)
        return left, line.reshape(grid_rows, -1)

    def wanted_by_row(labels):
        left, line = split_labels(labels)
        kept = labels[:, places_left + places_right :].reshape(
            grid_rows, grid_cols, rows_dev, retained_width
        )
        kept = lax.dynamic_index_in_dim(kept, col, 1, keepdims=False)
        inner_at = jnp.arange(KPB)
        keeps = flags(jnp.any(kept[:, :, :, None] == inner_at, axis=2))
        slot_a, col_a = split_label(left.transpose(2, 3, 0, 1, 4).reshape(grid_rows, grid_rows, -1))
        by_row = flags((slot_a // WA)[..., None] == jnp.arange(rows_dev))
        by_inner = flags(col_a[..., None] == inner_at)
        has = jnp.einsum("iker,ikeq->ikrq", by_row, by_inner, preferred_element_type=jnp.float32)
        uses = jnp.einsum(
            "ikrq,irj->kqij", has.astype(jnp.bfloat16), keeps, preferred_element_type=jnp.float32
        )
        slot_b, col_b = split_label(line)
        by_slot = flags((slot_b // WB)[..., None] == inner_at)
        found = jnp.einsum(
            "keq,kqij->keij", by_slot, flags(uses > 0.5), preferred_element_type=jnp.float32
        )
        found = jnp.sum(jnp.where(col_b[:, :, None, None] == inner_at, found, 0.0), axis=3)
        in_window = (rows_at[:, None] - rows_at[None, :] - col) % grid_rows < STEPS
        wanted = (found > 0.5) & in_window[:, None, :]
        wanted = wanted.transpose(2, 0, 1).reshape(grid_rows, -1)
        return jnp.stack([wanted, wanted[::-1]])

    def queues(places, capacity, arrived):
        into = jnp.stack(
            [
                lax.dynamic_index_in_dim(places[at], jnp.maximum(self_at[at] - 1, 0), 0, False)
                for at in range(2)
            ]
        )
        outof = jnp.stack(
            [
                lax.dynamic_index_in_dim(
                    places[at], jnp.minimum(self_at[at], grid_rows - 2), 0, False
                )
                for at in range(2)
            ]
        )
        come = jnp.stack(arrived(into))
        source = jnp.where(origins == self_at[:, None], place_home, come)
        hit = outof[:, None, :] == jnp.arange(capacity)[None, :, None]
        send = jnp.sum(jnp.where(hit, source[:, None, :], 0), axis=2)
        send = jnp.where((self_at < grid_rows - 1)[:, None], send, 0)
        lies = jnp.where(origins[0] <= row, source[0], come[1])
        return send, lies

    def products(lies, bounds, stage):
        left, line = split_labels(labels)
        slot_b, col_b = split_label(line)
        inner_at = jnp.arange(KPB)
        where_b = lies.reshape(grid_rows, -1)
        inner = (row + col + jnp.arange(STEPS)) % grid_rows
        slots = jnp.arange(slots_right)
        hit = jnp.take(slot_b, inner, axis=0)[:, None, :] == slots[:, None]
        b_at = jnp.sum(jnp.where(hit, jnp.take(where_b, inner, axis=0)[:, None, :], 0), axis=2)
        b_of = jnp.sum(jnp.where(hit, jnp.take(col_b, inner, axis=0)[:, None, :] + 1, 0), axis=2) - 1
        mine = lax.dynamic_index_in_dim(left, row, 2, keepdims=False)
        mine = jnp.take(mine, row ^ rows_at, axis=0)
        mine = jnp.take(mine, inner, axis=2).transpose(2, 1, 0, 3)
        slot_m, col_m = split_label(mine.reshape(STEPS, -1))
        base = jnp.arange(grid_cols)[:, None] * (places_left + 1)
        base = (base + rows_at * (grid_rows * depth_left)).reshape(1, -1, 1)
        a_place = base + inner[:, None, None] * depth_left + jnp.arange(depth_left)
        a_place = a_place.reshape(STEPS, -1)
        hit = slot_m[:, None, :] == jnp.arange(slots_left)[:, None]
        a_at = jnp.sum(jnp.where(hit, a_place[:, None, :], 0), axis=2)
        a_of = jnp.sum(jnp.where(hit, col_m[:, None, :] + 1, 0), axis=2) - 1
        meets = (a_of[:, :, None] == inner_at)[..., None]
        pair_at = jnp.sum(jnp.where(meets, b_at.reshape(STEPS, 1, KPB, WB), 0), axis=2)
        pair_of = jnp.sum(jnp.where(meets, b_of.reshape(STEPS, 1, KPB, WB) + 1, 0), axis=2) - 1
        kept = jnp.repeat(c_col, WA, axis=0)[None, :, None, :]
        same = (pair_of[..., None] == kept) & (kept >= 0)
        slot = jnp.sum(jnp.where(same, jnp.arange(retained_width) + 1, 0), axis=3) - 1
        target = (jnp.arange(slots_left) // WA)[None, :, None] * retained_width + slot
        left_code = (target * 2**23 + a_at[:, :, None] * 2**12).reshape(-1)
        spare = rows_dev * retained_width * 2**23
        valid = (slot >= 0).reshape(-1)
        pair_at = pair_at.reshape(-1)
        if bounds is None:
            return [compact(valid, left_code + pair_at, spare)]
        down = pair_at >= local + capacity
        arrived = jnp.where(down, pair_at - capacity, pair_at) - local
        part, offset = locate(arrived, bounds)
        late = (part >= stage) & (arrived >= 0)
        rounds = len(bounds) - 1
        early_code = jnp.where(
            arrived < 0, pair_at, (part + 1 + jnp.where(down, stage, 0)) * 128 + offset
        )
        late_code = (part - stage + jnp.where(down, rounds - stage, 0)) * 128 + offset
        return [
            compact(valid & ~late, left_code + early_code, spare),
            compact(valid & late, left_code + late_code, spare),
        ]

    def plan(labels):
        places = queue_places(
            wanted_by_row(labels), origins, lambda place: available(place, ROUNDS, LAG)
        )
        send, lies = queues(
            places, capacity, lambda into: (local + into[0], local + capacity + into[1])
        )
        send = jnp.where(send >= local + capacity, send - capacity, send)
        part, offset = locate(send - local, starts)
        send = jnp.where(send < local, send, (part + 1) * 128 + offset)
        return send, lies, jnp.max(places) + 1

    send, lies, longest = one_turn(plan, hold(labels))
    longest = jnp.broadcast_to(longest.astype(jnp.float32), (1, edge, edge))
    home_right, send, longest, *home = lax.optimization_barrier((home_right, send, longest, *home))
    home_left = join([*home, longest])
    early, late = products(lies, starts, STAGE)
    left = lax.all_gather(home_left, "col", tiled=True)
    stride = home_left.shape[0]
    longest = jnp.max(left[stride - 1 :: stride, 0, 0]).astype(jnp.int32)
    kept_blocks = rows_dev * retained_width

    def send_round(at, ups, downs):
        seen = max(at - LAG + 1, 0)
        codes = send[:, int(starts[at]) : int(starts[at + 1])]
        go_up, go_down = pack_round(codes, home_right, ups[:seen], downs[:seen], WEIGHT * (at == 1))
        return lax.ppermute(go_up, "row", up), lax.ppermute(go_down, "row", down)

    ups, downs = [], []
    for at in range(len(ROUNDS) - 1):
        came_up, came_down = send_round(at, ups, downs)
        ups.append(came_up)
        downs.append(came_down)
    total = multiply(*early, left, [home_right] + ups[:STAGE] + downs[:STAGE], kept_blocks)

    def finished(last_up, last_down):
        rights = [*ups[STAGE:], last_up, *downs[STAGE:], last_down]
        return multiply(*late, left, rights, kept_blocks, total)

    def usual():
        return finished(ups[-1], downs[-1])

    def longer():
        return finished(*send_round(len(ROUNDS) - 1, ups, downs))

    def looped():
        most = min((grid_rows - 1) * local, grid_rows * slots_right) + LOOP_ROUND * grid_rows
        most = -(-most // LOOP_ROUND) * LOOP_ROUND
        shared = most + LOOP_ROUND * (grid_rows + 1)
        end = local + shared
        places = queue_places(
            wanted_by_row(labels), origins, lambda place: (place // LOOP_ROUND + 1) * LOOP_ROUND
        )

        def from_end(place):
            return end - (place // LOOP_ROUND + 1) * LOOP_ROUND + place % LOOP_ROUND

        send, lies = queues(places, most, lambda into: (local + into[0], from_end(into[1])))
        rounds = (lax.pmax(jnp.max(places), ("row", "col")) + LOOP_ROUND) // LOOP_ROUND
        mine = [
            jnp.max(
                lax.dynamic_index_in_dim(places[at], jnp.maximum(self_at[at] - 1, 0), 0, False)
            )
            for at in range(2)
        ]
        mine = [jnp.where(self_at[at] > 0, mine[at], -1) for at in range(2)]
        ((codes, count),) = products(lies, None, None)
        store = jnp.zeros((end + LOOP_ROUND, edge, edge), jnp.float32)
        store = lax.dynamic_update_slice(store, home_right, (0, 0, 0))

        def one(at, store):
            index = lax.dynamic_slice(send, (0, at * LOOP_ROUND), (2, LOOP_ROUND))
            came = [
                lax.ppermute(jnp.take(store, index[side], axis=0, mode="clip"), "row", pairs)
                for side, pairs in ((0, up), (1, down))
            ]
            first = at * LOOP_ROUND
            for side, to in ((0, local + first), (1, end - first - LOOP_ROUND)):
                to = jnp.where(first <= mine[side], to, end)
                store = lax.dynamic_update_slice(store, came[side], (to, 0, 0))
            return store

        store = lax.fori_loop(0, rounds, one, store)
        return multiply(codes, count, left, [store], kept_blocks)

    usual_length = int(starts[-2])
    level = (longest > usual_length).astype(jnp.int32) + (longest > capacity).astype(jnp.int32)
    result = lax.switch(level, [usual, longer, looped])
    return result.reshape(rows_dev, retained_width, edge, edge)


def solution(mesh):
    return jax.shard_map(
        on_device,
        mesh=mesh,
        in_specs=(
            P(("row", "col"), None, None),
            P(("row", "col")),
            P(("row", "col")),
            P(("row", "col"), None, None),
            P(("row", "col")),
            P(("row", "col")),
            P("row", "col"),
        ),
        out_specs=P("row", "col", None, None),
        check_vma=False,
    )
```
